32 devices in a mesh: groups: 2 (over y), ctx: 16 (over z, x, core).
Axes of the slice: x: 2, y: 2, z: 4, core: 2. Of those that a mesh axis runs over, the one named last changes fastest.
Arguments:
- reduced_rows: bfloat16 [8192, 1024], P(('groups', 'ctx')), parts along dimension 0, may hold values from -40 to 40
- query_weight: bfloat16 [1024, 4096], replicated, may hold values from -1 to 1
- key_matrix: bfloat16 [1024, 512], replicated, may hold values from -1 to 1
- value_matrix: bfloat16 [1024, 512], replicated, may hold values from -0.1875 to 0.1875
- doc_flags: int32 [64], P(('groups', 'ctx')), parts along dimension 0, may hold values from 0 to 1, as said below
Outputs:
- context: bfloat16 [8192, 4096], P(('groups', 'ctx')), parts along dimension 0
The draws below stay inside these ranges and needn't reach their ends.
There are 2 independent parts, one for each index of `groups`. The reference program is written for one: setup_inputs(seed, part) draws one part's arguments, and reference() takes and returns one part's arrays. A program takes and returns all parts, laid end to end along the dimension named above; an argument that names none is the same for every part. Nothing has to cross between parts.
Inputs may be any that keep to these rules, and one draw needn't show every extreme that they name: `doc_flags`: tile 0 is a document of one tile; the document that begins at tile 1 holds exactly 2048 tokens; every document holds at most 2048 tokens.
All inputs are finite; a program needn't handle non-finite values.
Results may differ from the reference program's by a relative error of at most 0.012.
The reference program's roundings to bfloat16 on the way count: a program that leaves them out, or rounds other values in their place, can miss the bound.
Values may be sent and summed in bfloat16 or wider, within the bound.
A program may use at most 64 MiB of HBM per device.

```python
import math
import jax
import jax.numpy as jnp
from jax import lax

DEVICE_TOKENS = 256
TILE = 128
RANK_SIZE = 1024
QUERY_HEADS = 32
KEY_VALUE_HEADS = 4
HEAD_WIDTH = 128
SEQUENCE_TOKENS = 4096
MAXDOC = 2048


def shared_keys(key):
    return jax.random.normal(key, (RANK_SIZE, KEY_VALUE_HEADS * HEAD_WIDTH), jnp.float32) / math.sqrt(RANK_SIZE)


def draw_key_matrix(key, part):
    unrotated_keys = shared_keys(key)
    return unrotated_keys.astype(jnp.bfloat16)


def draw_query_weight(key, part):
    key = jax.random.fold_in(key, 5)
    noise_part = jax.random.normal(key, (RANK_SIZE, QUERY_HEADS * HEAD_WIDTH), jnp.float32) / math.sqrt(RANK_SIZE)
    return noise_part.astype(jnp.bfloat16)


def draw_reduced_rows(key, part):
    key = jax.random.fold_in(key, 7)
    key_one = jax.random.fold_in(key, 0)
    boosted = jax.random.normal(key_one, (SEQUENCE_TOKENS, RANK_SIZE), jnp.float32)
    return boosted.astype(jnp.bfloat16)


def draw_doc_flags(key, part):
    key = jax.random.fold_in(jax.random.fold_in(key, 11), part)
    tile_count = SEQUENCE_TOKENS // TILE
    longest = MAXDOC // TILE
    tile_ids = jnp.arange(tile_count, dtype=jnp.int32)
    coins = jax.random.randint(key, (tile_count,), 0, 4, dtype=jnp.int32)
    fresh = jnp.where(coins == 0, 1, 0).astype(jnp.int32)
    shifted = jnp.maximum(tile_ids - 1, 0)
    forced = jnp.where((tile_ids == 0) | (tile_ids >= 1) & (shifted % longest == 0), 1, 0).astype(jnp.int32)
    return jnp.where(tile_ids <= longest, forced, jnp.maximum(forced, fresh)).astype(jnp.int32)


def gaussian(stream_key, shape, deviation, most, held_as=jnp.bfloat16):
    drawn = jax.random.normal(stream_key, shape, jnp.float32) * deviation
    return jnp.minimum(jnp.maximum(drawn, -most), most).astype(held_as)


def setup_inputs(seed: int = 0, part: int = 0) -> dict:
    keys = jax.random.split(jax.random.key(seed), 6)
    part_keys = jax.random.split(jax.random.fold_in(keys[5], part), 6)
    reduced_rows = draw_reduced_rows(jax.random.fold_in(jax.random.fold_in(keys[5], part), 71), part)
    query_weight = draw_query_weight(jax.random.fold_in(keys[5], 71), part)
    key_matrix = draw_key_matrix(jax.random.fold_in(keys[5], 71), part)
    value_matrix = gaussian(keys[3], (RANK_SIZE, KEY_VALUE_HEADS * HEAD_WIDTH), RANK_SIZE ** -0.5, 0.1875)
    doc_flags = draw_doc_flags(jax.random.fold_in(jax.random.fold_in(keys[5], part), 71), part)
    return {"reduced_rows": reduced_rows, "query_weight": query_weight, "key_matrix": key_matrix, "value_matrix": value_matrix, "doc_flags": doc_flags}


ROPE_BASE = 500000.0
NEG_FLOOR = -1e+30

def apply_rotary(vectors, token_positions):
    half_dim = vectors.shape[-1] // 2
    freq_idx = jnp.arange(half_dim, dtype=jnp.float32)
    frequency = ROPE_BASE ** (-2.0 * freq_idx / vectors.shape[-1])
    angles = token_positions.astype(jnp.float32)[:, None] * frequency[None, :]
    cosine = jnp.cos(angles)[:, None, :]
    sine_vals = jnp.sin(angles)[:, None, :]
    front_half = vectors[..., :half_dim]
    back_half = vectors[..., half_dim:]
    return jnp.concatenate([front_half * cosine - back_half * sine_vals, back_half * cosine + front_half * sine_vals], axis=-1)

def reference(reduced_rows, query_weight, key_matrix, value_matrix, doc_flags):
    query_group_size = QUERY_HEADS // KEY_VALUE_HEADS
    tile_count = doc_flags.shape[0]
    tile_ids = jnp.arange(tile_count, dtype=jnp.int32)
    tile_start = lax.cummax(jnp.where(doc_flags == 1, tile_ids, -1).astype(jnp.int32), axis=0)
    doc_start = jnp.repeat(tile_start * TILE, TILE, total_repeat_length=SEQUENCE_TOKENS).astype(jnp.int32)
    token_positions = jnp.arange(SEQUENCE_TOKENS, dtype=jnp.int32)
    query_rows = apply_rotary(jnp.dot(reduced_rows, query_weight, preferred_element_type=jnp.float32).reshape(SEQUENCE_TOKENS, QUERY_HEADS, HEAD_WIDTH), token_positions).astype(jnp.bfloat16)
    key_matrix_rows = apply_rotary(jnp.dot(reduced_rows, key_matrix, preferred_element_type=jnp.float32).reshape(SEQUENCE_TOKENS, KEY_VALUE_HEADS, HEAD_WIDTH), token_positions).astype(jnp.bfloat16)
    value_matrix_rows = jnp.dot(reduced_rows, value_matrix, preferred_element_type=jnp.float32).astype(jnp.bfloat16).reshape(SEQUENCE_TOKENS, KEY_VALUE_HEADS, HEAD_WIDTH)
    padding_margin = MAXDOC - DEVICE_TOKENS
    padded_keys = jnp.concatenate([jnp.zeros((padding_margin, KEY_VALUE_HEADS, HEAD_WIDTH), jnp.bfloat16), key_matrix_rows], axis=0)
    padded_values = jnp.concatenate([jnp.zeros((padding_margin, KEY_VALUE_HEADS, HEAD_WIDTH), jnp.bfloat16), value_matrix_rows], axis=0)
    score_scale = 1.0 / math.sqrt(HEAD_WIDTH)

    def one_block(block_idx):
        block_offset = (block_idx * DEVICE_TOKENS).astype(jnp.int32)
        query_slice = lax.dynamic_slice_in_dim(query_rows, block_offset, DEVICE_TOKENS, 0).astype(jnp.float32).reshape(DEVICE_TOKENS, KEY_VALUE_HEADS, query_group_size, HEAD_WIDTH)
        key_block = lax.dynamic_slice_in_dim(padded_keys, block_offset, MAXDOC, 0).astype(jnp.float32)
        value_block = lax.dynamic_slice_in_dim(padded_values, block_offset, MAXDOC, 0).astype(jnp.float32)
        query_pos = block_offset + jnp.arange(DEVICE_TOKENS, dtype=jnp.int32)
        key_pos = block_offset - padding_margin + jnp.arange(MAXDOC, dtype=jnp.int32)
        row_starts = lax.dynamic_slice_in_dim(doc_start, block_offset, DEVICE_TOKENS, 0)
        visible = (key_pos[None, :] <= query_pos[:, None]) & (key_pos[None, :] >= row_starts[:, None])
        scores = jnp.einsum('qhgd,khd->hgqk', query_slice, key_block) * score_scale
        masked = jnp.where(visible, scores, NEG_FLOOR)
        row_top = lax.optimization_barrier(jnp.max(masked, axis=-1, keepdims=True))
        weights = jnp.where(visible, jnp.exp(masked - row_top), 0.0)
        row_total = lax.optimization_barrier(jnp.sum(weights, axis=-1))
        rounded = lax.optimization_barrier(weights.astype(jnp.bfloat16)).astype(jnp.float32)
        mixed_sum = jnp.einsum('hgqk,khd->hgqd', rounded, value_block)
        context = mixed_sum / row_total[..., None]
        return jnp.transpose(context, (2, 0, 1, 3)).reshape(DEVICE_TOKENS, QUERY_HEADS * HEAD_WIDTH).astype(jnp.bfloat16)
    block_out = lax.map(one_block, jnp.arange(SEQUENCE_TOKENS // DEVICE_TOKENS, dtype=jnp.int32))
    return block_out.reshape(SEQUENCE_TOKENS, QUERY_HEADS * HEAD_WIDTH)
```

```python
import functools
import math

import jax
import jax.numpy as jnp
import numpy as np
from jax import lax
from jax.experimental import pallas as pl
from jax.experimental.pallas import tpu as pltpu

TILE = 128
MAXDOC = 2048
HEAD = 128
ROPE_BASE = 500000.0
NEG = -1e30
MARK_ROWS = 16


def needed(source, target):
    edge = MAXDOC // TILE // 4
    return (source >= 0) & ((source >= edge) | (target <= edge))


def kernel(
    chips, group, flags_ref, x_ref, wk_ref, wv_ref, cos_ref, sin_ref, freq_ref, wq_hbm, out_hbm,
    kv, send, xs, wq, queries, top, mix, bias_own, blocked, staged, cosine, sine,
    wq_sem, x_send, x_recv, kv_send, kv_recv, out_sem, out_send, out_recv,
):
    me = lax.axis_index("ctx")
    chip, core = me // 2, me % 2
    other = 1 - core
    sibling = chip * 2 + other
    tok = x_ref.shape[0]
    half = wq.shape[1]
    scale = math.log2(math.e) / math.sqrt(HEAD)

    wq_copy = pltpu.make_async_copy(
        wq_hbm.at[:, pl.ds(pl.multiple_of(core * half, half), half)], wq, wq_sem
    )
    wq_copy.start()

    barrier = pltpu.get_barrier_semaphore()
    pl.semaphore_signal(barrier, inc=1, device_id={"ctx": sibling})
    for hop in range(1, 5):
        @pl.when(needed(chip - hop, chip))
        def _():
            for c in range(2) if hop < 4 else (1,):
                pl.semaphore_signal(barrier, inc=1, device_id={"ctx": (chip - hop) * 2 + c})

    def sends_to(hop):
        fits = (chip + hop < chips) & needed(chip, chip + hop)
        return fits if hop < 4 else fits & (core == 1)

    base = (chip * (2 * tok)).astype(jnp.float32) * freq_ref[...]
    cos_b, sin_b = jnp.cos(base)[:1], jnp.sin(base)[:1]
    sign = jnp.where(lax.broadcasted_iota(jnp.int32, (1, HEAD), 1) < HEAD // 2, -1.0, 1.0)
    cosine[...] = cos_ref[...] * cos_b - sin_ref[...] * sin_b
    sine[...] = (sin_ref[...] * cos_b + cos_ref[...] * sin_b) * sign

    def rope(v, cs, sn):
        return v * cs + pltpu.roll(v, HEAD // 2, 1) * sn

    own = pl.ds(pl.multiple_of(core * tok, tok), tok)
    x = x_ref[...]
    cs, sn = cosine[own, :], sine[own, :]
    heads = wk_ref.shape[1] // HEAD // 2
    flag_rows = jnp.where(
        lax.broadcasted_iota(jnp.int32, (MARK_ROWS, HEAD), 0) < MARK_ROWS // 2, flags_ref[0], flags_ref[1]
    ).astype(jnp.float32).astype(jnp.bfloat16)
    for part in range(2):
        cols = slice(part * heads * HEAD, (part + 1) * heads * HEAD)
        ks = jnp.dot(x, wk_ref[:, cols], preferred_element_type=jnp.float32)
        vs = jnp.dot(x, wv_ref[:, cols], preferred_element_type=jnp.float32)
        for h in range(heads):
            hc = slice(h * HEAD, (h + 1) * HEAD)
            send[part, 2 * h * tok:(2 * h + 1) * tok, :] = rope(ks[:, hc], cs, sn).astype(jnp.bfloat16)
            send[part, (2 * h + 1) * tok:(2 * h + 2) * tok, :] = vs[:, hc].astype(jnp.bfloat16)
        send[part, 2 * heads * tok:, :] = flag_rows

    targets = sum(sends_to(hop).astype(jnp.int32) for hop in range(1, 5))
    pl.semaphore_wait(barrier, 1 + 2 * targets)

    def kv_copy(hop, part):
        return pltpu.make_async_remote_copy(
            src_ref=send.at[part], dst_ref=kv.at[hop, core],
            send_sem=kv_send.at[hop, part], recv_sem=kv_recv.at[hop, core],
            device_id={"ctx": (chip + hop) * 2 + part},
        )

    def own_copy():
        return pltpu.make_async_remote_copy(
            src_ref=send.at[other], dst_ref=kv.at[0, core],
            send_sem=kv_send.at[0, 0], recv_sem=kv_recv.at[0, core],
            device_id={"ctx": sibling},
        )

    x_copy = pltpu.make_async_remote_copy(
        src_ref=x_ref, dst_ref=xs.at[core], send_sem=x_send, recv_sem=x_recv, device_id={"ctx": sibling},
    )
    x_copy.start()
    own_copy().start()
    for hop in range(1, 5):
        @pl.when(sends_to(hop))
        def _():
            for part in range(2):
                kv_copy(hop, part).start()
    xs[core] = x
    kv[0, core] = send[core]

    x_copy.wait()
    wq_copy.wait()
    pairs = half // (2 * HEAD)
    tiles = 2 * tok // TILE

    @pl.loop(0, pairs)
    def _(pair):
        kvh, hp = pair // (group // 2), pair % (group // 2)
        w = wq[:, pl.ds(pl.multiple_of(pair * 2 * HEAD, 2 * HEAD), 2 * HEAD)]
        for c in range(2):
            q = jnp.dot(xs[c], w, preferred_element_type=jnp.float32)
            for e in range(2):
                r = rope(
                    q[:, e * HEAD:(e + 1) * HEAD], cosine[c * tok:(c + 1) * tok, :], sine[c * tok:(c + 1) * tok, :]
                ).astype(jnp.bfloat16)
                for t in range(tok // TILE):
                    queries[
                        kvh, c * (tok // TILE) + t, pl.ds(pl.multiple_of((hp * 2 + e) * TILE, TILE), TILE), :
                    ] = r[t * TILE:(t + 1) * TILE]

    def marks(hop, c):
        rows = kv[hop, c, 2 * heads * tok:, :].astype(jnp.float32)
        return [rows[0:1], rows[MARK_ROWS // 2:MARK_ROWS // 2 + 1]]

    chunk = 2 * TILE

    def attend(hop, unit_tiles, cores, bias_of, first):
        @pl.loop(0, heads * unit_tiles)
        def _(unit):
            h, i = unit // unit_tiles, unit % unit_tiles
            k0 = pl.multiple_of(h * 2 * tok, tok)
            v0 = pl.multiple_of(h * 2 * tok + tok, tok)
            k = jnp.concatenate([kv[hop, c, pl.ds(k0, tok), :] for c in cores], axis=0)
            v = jnp.concatenate([kv[hop, c, pl.ds(v0, tok), :] for c in cores], axis=0)
            v = jnp.concatenate([v, jnp.ones_like(v)], axis=1)
            bias = bias_of(i)
            for r in range(group * TILE // chunk):
                rows = slice(r * chunk, (r + 1) * chunk)
                s = lax.dot_general(
                    queries[h, i, rows, :], k, (((1,), (1,)), ((), ())), preferred_element_type=jnp.float32
                )
                s = s + bias
                highest = jnp.max(s, axis=1, keepdims=True)
                if first:
                    new = jnp.broadcast_to(highest, (chunk, HEAD))
                else:
                    old = top[h, i, rows, :]
                    new = jnp.maximum(old, highest)
                wide = jnp.concatenate([new] * (s.shape[1] // HEAD), axis=1)
                p = jnp.exp2((s - wide) * scale).astype(jnp.bfloat16)
                o = jnp.dot(p, v, preferred_element_type=jnp.float32)
                if not first:
                    factor = jnp.exp2((old - new) * scale)
                    o = o + mix[h, i, rows, :] * jnp.concatenate([factor, factor], axis=1)
                mix[h, i, rows, :] = o
                top[h, i, rows, :] = new

    own_copy().wait_send()
    pltpu.make_async_remote_copy(
        src_ref=send.at[other], dst_ref=kv.at[0, other], send_sem=kv_send.at[0, 0],
        recv_sem=kv_recv.at[0, other], device_id={"ctx": sibling},
    ).wait_recv()
    flags = marks(0, 0) + marks(0, 1)
    row = lax.broadcasted_iota(jnp.int32, (TILE, TILE), 0)
    col = lax.broadcasted_iota(jnp.int32, (TILE, TILE), 1)
    causal = jnp.where(col <= row, 0.0, NEG)
    for i in range(tiles):
        seen = jnp.zeros((1, HEAD), jnp.float32)
        for j in reversed(range(tiles)):
            cols = slice(j * TILE, (j + 1) * TILE)
            if j > i:
                bias_own[i, :, cols] = jnp.full((TILE, TILE), NEG, jnp.float32)
            elif j == i:
                bias_own[i, :, cols] = causal
                seen = flags[j]
            else:
                bias_own[i, :, cols] = jnp.broadcast_to(seen * NEG, (TILE, TILE))
                seen = jnp.maximum(seen, flags[j])
        blocked[i] = jnp.broadcast_to(seen, (8, HEAD))

    def own_bias(i):
        b = bias_own[i]
        return jnp.concatenate([b] * (chunk // TILE), axis=0)

    attend(0, tiles, (0, 1), own_bias, True)

    def far_bias(i, cores, hop):
        seen = blocked[i][0:1]
        cols = []
        for c in reversed(cores):
            for f in reversed(marks(hop, c)):
                cols.insert(0, seen * NEG)
                seen = jnp.maximum(seen, f)
        return jnp.concatenate(cols, axis=1), seen

    for hop in range(1, 5):
        cores = (0, 1) if hop < 4 else (1,)
        unit_tiles = tiles if hop < 4 else tiles // 2

        @pl.when(needed(chip - hop, chip))
        def _():
            for c in cores:
                pltpu.make_async_remote_copy(
                    src_ref=send.at[0], dst_ref=kv.at[hop, c], send_sem=kv_send.at[hop, 0],
                    recv_sem=kv_recv.at[hop, c], device_id={"ctx": sibling},
                ).wait_recv()
            attend(hop, unit_tiles, cores, lambda i: far_bias(i, cores, hop)[0], False)
            if hop < 4:
                for i in range(tiles):
                    blocked[i] = jnp.broadcast_to(far_bias(i, cores, hop)[1], (8, HEAD))

    @pl.loop(0, heads * tiles)
    def _(unit):
        h, i = unit // tiles, unit % tiles
        for r in range(group):
            rows = slice(r * TILE, (r + 1) * TILE)
            a = mix[h, i, rows, :]
            staged[
                pl.ds(pl.multiple_of(i * TILE, TILE), TILE),
                pl.ds(pl.multiple_of((h * group + r) * HEAD, HEAD), HEAD),
            ] = (a[:, :HEAD] / a[:, HEAD:]).astype(jnp.bfloat16)

    my_cols = pl.ds(pl.multiple_of(core * half, half), half)
    their_rows = pl.ds(pl.multiple_of(other * tok, tok), tok)
    out_remote = pltpu.make_async_remote_copy(
        src_ref=staged.at[their_rows, :], dst_ref=out_hbm.at[:, my_cols],
        send_sem=out_send, recv_sem=out_recv, device_id={"ctx": sibling},
    )
    out_remote.start()
    out_local = pltpu.make_async_copy(staged.at[own, :], out_hbm.at[:, my_cols], out_sem)
    out_local.start()
    for hop in range(1, 5):
        @pl.when(sends_to(hop))
        def _():
            for part in range(2):
                kv_copy(hop, part).wait_send()
    out_local.wait()
    out_remote.wait()


def local(chips, reduced_rows, query_weight, key_matrix, value_matrix, doc_flags):
    tok, rank = reduced_rows.shape
    q_width = query_weight.shape[1]
    kv_heads = key_matrix.shape[1] // HEAD
    group = q_width // HEAD // kv_heads
    half, heads = q_width // 2, kv_heads // 2
    tiles = 2 * tok // TILE
    slab = 2 * heads * tok + MARK_ROWS
    m = np.arange(HEAD // 2, dtype=np.float64)
    freq = ROPE_BASE ** (-2.0 * m / HEAD)
    freq = np.concatenate([freq, freq])
    angles = np.arange(2 * tok, dtype=np.float64)[:, None] * freq[None, :]
    vmem = pl.BlockSpec(memory_space=pltpu.VMEM)
    bf, f32 = jnp.bfloat16, jnp.float32
    dma = pltpu.SemaphoreType.DMA
    return pl.pallas_call(
        functools.partial(kernel, chips, group),
        out_shape=jax.ShapeDtypeStruct((tok, q_width), bf),
        in_specs=[pl.BlockSpec(memory_space=pltpu.SMEM)] + [vmem] * 6 + [pl.BlockSpec(memory_space=pl.ANY)],
        out_specs=pl.BlockSpec(memory_space=pl.ANY),
        scratch_shapes=[
            pltpu.VMEM((5, 2, slab, HEAD), bf),
            pltpu.VMEM((2, slab, HEAD), bf),
            pltpu.VMEM((2, tok, rank), bf),
            pltpu.VMEM((rank, half), bf),
            pltpu.VMEM((heads, tiles, group * TILE, HEAD), bf),
            pltpu.VMEM((heads, tiles, group * TILE, HEAD), f32),
            pltpu.VMEM((heads, tiles, group * TILE, 2 * HEAD), f32),
            pltpu.VMEM((tiles, TILE, tiles * TILE), f32),
            pltpu.VMEM((tiles, 8, HEAD), f32),
            pltpu.VMEM((2 * tok, half), bf),
            pltpu.VMEM((2 * tok, HEAD), f32),
            pltpu.VMEM((2 * tok, HEAD), f32),
            dma, dma, dma, dma((5, 2)), dma((5, 2)), dma, dma, dma,
        ],
        compiler_params=pltpu.CompilerParams(
            collective_id=0, has_side_effects=True, vmem_limit_bytes=56 * 1024 * 1024
        ),
        cost_estimate=pl.CostEstimate(flops=12 * 10**9, bytes_accessed=12 * 10**6, transcendentals=16 * 10**6),
    )(
        doc_flags, reduced_rows, key_matrix, value_matrix,
        jnp.asarray(np.cos(angles), f32), jnp.asarray(np.sin(angles), f32),
        jnp.asarray(np.broadcast_to(freq, (8, HEAD)), f32), query_weight,
    )


def solution(mesh):
    chips = mesh.shape["ctx"] // 2
    in_specs = (P(("groups", "ctx"), None), P(), P(), P(), P(("groups", "ctx")))
    return jax.shard_map(
        functools.partial(local, chips), mesh=mesh, in_specs=in_specs,
        out_specs=P(("groups", "ctx"), None), check_vma=False,
    )


P = jax.sharding.PartitionSpec
```

```python
import functools
import math

import jax
import jax.numpy as jnp
import numpy as np
from jax import lax
from jax.experimental import pallas as pl
from jax.experimental.pallas import tpu as pltpu

TILE = 128
MAXDOC = 2048
HEAD = 128
ROPE_BASE = 500000.0
NEG = -1e30
CHUNK = 256
AHEAD = 1
MARK_ROWS = 16
RELAY = 2


def needed(source, target):
    return (source >= 0) & ((source >= EDGE) | (target <= EDGE))


EDGE = MAXDOC // TILE // 4


def sends(source, hop, chips):
    target = source + hop
    direct = needed(source, target) & ((target != EDGE) | (hop == EDGE - RELAY))
    return (target < chips) & (direct | ((source == EDGE - 1) & (hop == 2)))


def kernel(
    chips, group, flags_ref, x_ref, wk_ref, wv_ref, cos_ref, sin_ref, freq_ref, wq_hbm, out_hbm,
    kv, send, xs, wq, queries, top, mix, bias_own, onehot, blocked, staged, cosine, sine,
    wq_sem, x_send, x_recv, kv_send, kv_recv, relay_send, out_sem, out_send, out_recv,
):
    me = lax.axis_index("ctx")
    chip, core = me // 2, me % 2
    other = 1 - core
    sibling = chip * 2 + other
    tok = x_ref.shape[0]
    half = wq.shape[1]
    tiles = 2 * tok // TILE
    scale = math.log2(math.e) / math.sqrt(HEAD)

    wq_copy = pltpu.make_async_copy(
        wq_hbm.at[:, pl.ds(pl.multiple_of(core * half, half), half)], wq, wq_sem
    )
    wq_copy.start()

    barrier = pltpu.get_barrier_semaphore()
    pl.semaphore_signal(barrier, inc=1, device_id={"ctx": sibling})
    for hop in range(1, 5):
        @pl.when((chip >= hop) & sends(chip - hop, hop, chips))
        def _():
            for c in range(2) if hop < 4 else (1,):
                pl.semaphore_signal(barrier, inc=1, device_id={"ctx": (chip - hop) * 2 + c})

    @pl.when(chip == EDGE)
    def _():
        pl.semaphore_signal(barrier, inc=1, device_id={"ctx": (EDGE + 1) * 2 + core})

    def sends_to(hop):
        fits = sends(chip, hop, chips)
        return fits if hop < 4 else fits & (core == 1)

    base = (chip * (2 * tok)).astype(jnp.float32) * freq_ref[...]
    cos_b, sin_b = jnp.cos(base)[:1], jnp.sin(base)[:1]
    sign = jnp.where(lax.broadcasted_iota(jnp.int32, (1, HEAD), 1) < HEAD // 2, -1.0, 1.0)
    cosine[...] = cos_ref[...] * cos_b - sin_ref[...] * sin_b
    sine[...] = (sin_ref[...] * cos_b + cos_ref[...] * sin_b) * sign

    def rope(v, cs, sn):
        return v * cs + pltpu.roll(v, HEAD // 2, 1) * sn

    own = pl.ds(pl.multiple_of(core * tok, tok), tok)
    x = x_ref[...]
    cs, sn = cosine[own, :], sine[own, :]
    heads = wk_ref.shape[1] // HEAD // 2
    flag_rows = jnp.where(
        lax.broadcasted_iota(jnp.int32, (MARK_ROWS, HEAD), 0) < MARK_ROWS // 2, flags_ref[0], flags_ref[1]
    ).astype(jnp.float32).astype(jnp.bfloat16)
    for part in range(2):
        cols = slice(part * heads * HEAD, (part + 1) * heads * HEAD)
        ks = jnp.dot(x, wk_ref[:, cols], preferred_element_type=jnp.float32)
        vs = jnp.dot(x, wv_ref[:, cols], preferred_element_type=jnp.float32)
        for h in range(heads):
            hc = slice(h * HEAD, (h + 1) * HEAD)
            turned = rope(ks[:, hc], cs, sn).astype(jnp.bfloat16)
            for t in range(tok // TILE):
                send[part, 2 * h * tok + t * TILE:2 * h * tok + (t + 1) * TILE, :] = turned[t * TILE:(t + 1) * TILE].T
            send[part, (2 * h + 1) * tok:(2 * h + 2) * tok, :] = vs[:, hc].astype(jnp.bfloat16)
        send[part, 2 * heads * tok:, :] = flag_rows

    targets = sum(sends_to(hop).astype(jnp.int32) for hop in range(1, 5))
    pl.semaphore_wait(barrier, 1 + 2 * targets + (chip == EDGE + 1).astype(jnp.int32))

    def kv_copy(hop, part):
        return pltpu.make_async_remote_copy(
            src_ref=send.at[part], dst_ref=kv.at[hop, core],
            send_sem=kv_send.at[hop, part], recv_sem=kv_recv.at[hop, core],
            device_id={"ctx": (chip + hop) * 2 + part},
        )

    def relay_copy(index, from_hop, to_hop, c):
        return pltpu.make_async_remote_copy(
            src_ref=kv.at[from_hop, c], dst_ref=kv.at[to_hop, c],
            send_sem=relay_send.at[index], recv_sem=kv_recv.at[to_hop, c],
            device_id={"ctx": EDGE * 2 + core},
        )

    def arrived(hop, c):
        pltpu.make_async_remote_copy(
            src_ref=send.at[0], dst_ref=kv.at[hop, c], send_sem=kv_send.at[hop, 0],
            recv_sem=kv_recv.at[hop, c], device_id={"ctx": sibling},
        ).wait_recv()

    early = ((2, 4, 1), (1, 3, 0), (1, 3, 1))
    late = ((2, 1, 0), (2, 1, 1))

    def own_copy():
        return pltpu.make_async_remote_copy(
            src_ref=send.at[other], dst_ref=kv.at[0, core],
            send_sem=kv_send.at[0, 0], recv_sem=kv_recv.at[0, core],
            device_id={"ctx": sibling},
        )

    x_copy = pltpu.make_async_remote_copy(
        src_ref=x_ref, dst_ref=xs.at[core], send_sem=x_send, recv_sem=x_recv, device_id={"ctx": sibling},
    )
    x_copy.start()
    own_copy().start()
    for hop in range(1, 5):
        @pl.when(sends_to(hop))
        def _():
            for part in range(2):
                kv_copy(hop, part).start()
    xs[core] = x
    kv[0, core] = send[core]

    x_copy.wait()
    wq_copy.wait()
    pairs = half // (2 * HEAD)

    @pl.loop(0, pairs)
    def _(pair):
        kvh, hp = pair // (group // 2), pair % (group // 2)
        w = wq[:, pl.ds(pl.multiple_of(pair * 2 * HEAD, 2 * HEAD), 2 * HEAD)]
        q = jnp.dot(xs[...].reshape(2 * tok, -1), w, preferred_element_type=jnp.float32)
        for e in range(2):
            r = rope(q[:, e * HEAD:(e + 1) * HEAD], cosine[...], sine[...]).astype(jnp.bfloat16)
            for t in range(tiles):
                queries[kvh, t, pl.ds(pl.multiple_of((hp * 2 + e) * TILE, TILE), TILE), :] = (
                    r[t * TILE:(t + 1) * TILE]
                )

    def marks(hop, c):
        rows = kv[hop, c, 2 * heads * tok:, :].astype(jnp.float32)
        return [rows[0:1], rows[MARK_ROWS // 2:MARK_ROWS // 2 + 1]]

    chunk = CHUNK

    def attend(hop, i, cores, keys, bias, first):
        def slab(h):
            k0, v0 = h * 2 * tok, h * 2 * tok + tok
            k = jnp.concatenate(
                [kv[hop, c, k0 + t * TILE:k0 + (t + 1) * TILE, :] for c in cores for t in range(tok // TILE)], axis=1
            )[:, :keys]
            v = jnp.concatenate([kv[hop, c, v0:v0 + tok, :] for c in cores], axis=0)[:keys]
            return jnp.concatenate([k, bias], axis=0), jnp.concatenate([v, jnp.ones_like(v)], axis=1)

        slabs = [slab(h) for h in range(heads)]
        work = [(h, slice(r * chunk, (r + 1) * chunk)) for h in range(heads) for r in range(group * TILE // chunk)]

        def score(h, rows):
            return jnp.dot(
                jnp.concatenate([queries[h, i, rows, :], onehot[...]], axis=1), slabs[h][0],
                preferred_element_type=jnp.float32,
            )

        ahead = [score(*w) for w in work[:AHEAD]]
        for n, (h, rows) in enumerate(work):
            if n + AHEAD < len(work):
                ahead.append(score(*work[n + AHEAD]))
            s = ahead[n]
            highest = jnp.max(s, axis=1, keepdims=True)
            if first:
                new = jnp.broadcast_to(highest, (chunk, HEAD))
            else:
                old = top[h, i, rows, :]
                new = jnp.maximum(old, highest)
            wide = jnp.concatenate([new] * (keys // HEAD), axis=1)
            p = jnp.exp2((s - wide) * scale).astype(jnp.bfloat16)
            o = jnp.dot(p, slabs[h][1], preferred_element_type=jnp.float32)
            if not first:
                factor = jnp.exp2((old - new) * scale)
                o = o + mix[h, i, rows, :] * jnp.concatenate([factor, factor], axis=1)
            mix[h, i, rows, :] = o
            top[h, i, rows, :] = new

    onehot[...] = jnp.where(
        lax.broadcasted_iota(jnp.int32, onehot.shape, 0) % TILE == lax.broadcasted_iota(jnp.int32, onehot.shape, 1),
        1.0, 0.0,
    ).astype(jnp.bfloat16)

    own_copy().wait_send()
    pltpu.make_async_remote_copy(
        src_ref=send.at[other], dst_ref=kv.at[0, other], send_sem=kv_send.at[0, 0],
        recv_sem=kv_recv.at[0, other], device_id={"ctx": sibling},
    ).wait_recv()
    flags = marks(0, 0) + marks(0, 1)
    row = lax.broadcasted_iota(jnp.int32, (TILE, TILE), 0)
    key = lax.broadcasted_iota(jnp.int32, (TILE, TILE), 1)
    causal = jnp.where(key <= row, 0.0, NEG).astype(jnp.bfloat16)
    for i in range(tiles):
        seen = flags[i]
        bias_own[i, :, i * TILE:(i + 1) * TILE] = causal
        for j in reversed(range(i)):
            bias_own[i, :, j * TILE:(j + 1) * TILE] = jnp.broadcast_to(seen * NEG, (TILE, TILE)).astype(jnp.bfloat16)
            seen = jnp.maximum(seen, flags[j])
        blocked[i] = jnp.broadcast_to(seen, (8, HEAD))

    for i in range(tiles):
        keys = (i + 1) * TILE

        attend(0, i, (0, 1), keys, bias_own[i, :, :keys], True)

    @pl.when(chip == EDGE - RELAY)
    def _():
        for index, (here, there, c) in enumerate(early):
            arrived(here, c)
            relay_copy(index, here, there, c).start()
        arrived(2, 0)

    @pl.when(chip == EDGE + 1)
    def _():
        for index, (here, there, c) in enumerate(late):
            arrived(here, c)
            relay_copy(index, here, there, c).start()

    def far_bias(i, cores, hop):
        seen = blocked[i][0:1]
        blocks = []
        for c in reversed(cores):
            for f in reversed(marks(hop, c)):
                blocks.insert(0, jnp.broadcast_to(seen * NEG, (TILE, HEAD)).astype(jnp.bfloat16))
                seen = jnp.maximum(seen, f)
        return jnp.concatenate(blocks, axis=1), seen

    for hop in range(1, 5):
        cores = (0, 1) if hop < 4 else (1,)
        unit_tiles = tiles if hop < 4 else tiles // 2

        @pl.when(needed(chip - hop, chip))
        def _():
            @pl.when((chip != EDGE - RELAY) | (hop > 2))
            def _():
                for c in cores:
                    arrived(hop, c)


            @pl.loop(0, jnp.where(chip == EDGE, 1, unit_tiles))
            def _(i):
                attend(hop, i, cores, len(cores) * tok, far_bias(i, cores, hop)[0], False)

            if hop < 4:
                for i in range(tiles):
                    blocked[i] = jnp.broadcast_to(far_bias(i, cores, hop)[1], (8, HEAD))

    @pl.loop(0, heads * tiles)
    def _(unit):
        h, i = unit // tiles, unit % tiles
        for r in range(group):
            rows = slice(r * TILE, (r + 1) * TILE)
            a = mix[h, i, rows, :]
            staged[
                pl.ds(pl.multiple_of(i * TILE, TILE), TILE),
                pl.ds(pl.multiple_of((h * group + r) * HEAD, HEAD), HEAD),
            ] = (a[:, :HEAD] / a[:, HEAD:]).astype(jnp.bfloat16)

    my_cols = pl.ds(pl.multiple_of(core * half, half), half)
    their_rows = pl.ds(pl.multiple_of(other * tok, tok), tok)
    out_remote = pltpu.make_async_remote_copy(
        src_ref=staged.at[their_rows, :], dst_ref=out_hbm.at[:, my_cols],
        send_sem=out_send, recv_sem=out_recv, device_id={"ctx": sibling},
    )
    out_remote.start()
    out_local = pltpu.make_async_copy(staged.at[own, :], out_hbm.at[:, my_cols], out_sem)
    out_local.start()
    for hop in range(1, 5):
        @pl.when(sends_to(hop))
        def _():
            for part in range(2):
                kv_copy(hop, part).wait_send()
    for role, moves in ((EDGE - RELAY, early), (EDGE + 1, late)):
        @pl.when(chip == role)
        def _():
            for index, (here, there, c) in enumerate(moves):
                relay_copy(index, here, there, c).wait_send()
    out_local.wait()
    out_remote.wait()


def local(chips, reduced_rows, query_weight, key_matrix, value_matrix, doc_flags):
    tok, rank = reduced_rows.shape
    q_width = query_weight.shape[1]
    kv_heads = key_matrix.shape[1] // HEAD
    group = q_width // HEAD // kv_heads
    half, heads = q_width // 2, kv_heads // 2
    tiles = 2 * tok // TILE
    slab = 2 * heads * tok + MARK_ROWS
    m = np.arange(HEAD // 2, dtype=np.float64)
    freq = ROPE_BASE ** (-2.0 * m / HEAD)
    freq = np.concatenate([freq, freq])
    angles = np.arange(2 * tok, dtype=np.float64)[:, None] * freq[None, :]
    vmem = pl.BlockSpec(memory_space=pltpu.VMEM)
    bf, f32 = jnp.bfloat16, jnp.float32
    dma = pltpu.SemaphoreType.DMA
    return pl.pallas_call(
        functools.partial(kernel, chips, group),
        out_shape=jax.ShapeDtypeStruct((tok, q_width), bf),
        in_specs=[pl.BlockSpec(memory_space=pltpu.SMEM)] + [vmem] * 6 + [pl.BlockSpec(memory_space=pl.ANY)],
        out_specs=pl.BlockSpec(memory_space=pl.ANY),
        scratch_shapes=[
            pltpu.VMEM((5, 2, slab, HEAD), bf),
            pltpu.VMEM((2, slab, HEAD), bf),
            pltpu.VMEM((2, tok, rank), bf),
            pltpu.VMEM((rank, half), bf),
            pltpu.VMEM((heads, tiles, group * TILE, HEAD), bf),
            pltpu.VMEM((heads, tiles, group * TILE, HEAD), f32),
            pltpu.VMEM((heads, tiles, group * TILE, 2 * HEAD), f32),
            pltpu.VMEM((tiles, TILE, tiles * TILE), bf),
            pltpu.VMEM((CHUNK, TILE), bf),
            pltpu.VMEM((tiles, 8, HEAD), f32),
            pltpu.VMEM((2 * tok, half), bf),
            pltpu.VMEM((2 * tok, HEAD), f32),
            pltpu.VMEM((2 * tok, HEAD), f32),
            dma, dma, dma, dma((5, 2)), dma((5, 2)), dma((3,)), dma, dma, dma,
        ],
        compiler_params=pltpu.CompilerParams(
            collective_id=0, has_side_effects=True, vmem_limit_bytes=56 * 1024 * 1024
        ),
        cost_estimate=pl.CostEstimate(flops=12 * 10**9, bytes_accessed=12 * 10**6, transcendentals=16 * 10**6),
    )(
        doc_flags, reduced_rows, key_matrix, value_matrix,
        jnp.asarray(np.cos(angles), f32), jnp.asarray(np.sin(angles), f32),
        jnp.asarray(np.broadcast_to(freq, (8, HEAD)), f32), query_weight,
    )


def solution(mesh):
    chips = mesh.shape["ctx"] // 2
    in_specs = (P(("groups", "ctx"), None), P(), P(), P(), P(("groups", "ctx")))
    return jax.shard_map(
        functools.partial(local, chips), mesh=mesh, in_specs=in_specs,
        out_specs=P(("groups", "ctx"), None), check_vma=False,
    )


P = jax.sharding.PartitionSpec
```
